32 devices in a mesh: dom: 2 (over y), slab: 4 (over z), shift: 4 (over x, core).
Axes of the slice: x: 2, y: 2, z: 4, core: 2. Of those that a mesh axis runs over, the one named last changes fastest.
Arguments:
- subspace: float32 [16, 64, 512], P(None, ('dom', 'slab')), parts along dimension 1, may hold values from -6 to 6
- potential: float32 [64, 512], P(('dom', 'slab')), parts along dimension 0, may hold values from -2 to 2
- slow_shifts: int32 [4], P('dom'), parts along dimension 0, may hold values from 0 to 7, as said below
Outputs:
- filtered: float32 [16, 64, 512], P('shift', ('dom', 'slab')), parts along dimension 1
The draws below stay inside these ranges and needn't reach their ends.
There are 2 independent parts, one for each index of `dom`. The reference program is written for one: setup_inputs(seed, part) draws one part's arguments, and reference() takes and returns one part's arrays. A program takes and returns all parts, laid end to end along the dimension named above; each array names one. Nothing has to cross between parts.
Inputs may be any that keep to these rules, and one draw needn't show every extreme that they name: `slow_shifts`: two different shift numbers.
All inputs are finite; a program needn't handle non-finite values.
Results may differ from the reference program's by a relative error of at most 0.0003.
Values sent between devices are 32-bit elements; how exact they have to be, the bound alone decides.
A program may use at most 64 MiB of HBM per device.

```python
import math
import jax
import jax.numpy as jnp
from jax import lax

NS = 8
FAST = 2
SLOW = 4
LY = 32
PLANE = 512
NZ = 32
COLS = 16


def draw_slow_shifts(key, part):
    key = jax.random.fold_in(key, 5)
    first_key = jax.random.fold_in(key, 11)
    offset_key = jax.random.fold_in(key, 23)
    first = jax.random.randint(first_key, (), 0, NS)
    offset = jax.random.randint(offset_key, (), 1, NS)
    second = (first + offset) % NS
    return jnp.stack([first, second]).astype(jnp.int32)


def steps_of(key, dims, shards, least, top_value):
    def one(dim, shards_of):
        heights = jax.random.uniform(jax.random.fold_in(jax.random.fold_in(key, 6), dim), (shards_of,), jnp.float32, least / len(shards), top_value / len(shards))
        return jnp.repeat(jnp.exp(heights), dims[dim] // shards_of).reshape((-1,) + (1,) * (len(dims) - dim - 1))

    gain = one(*shards[0])
    for cut in shards[1:]:
        gain = gain * one(*cut)
    return gain


def normal_values(stream_key, extent, scale, reach, cuts=(), held_as=jnp.bfloat16):
    loudness = steps_of(stream_key, extent, cuts, -0.22, 0.18) if cuts else 1.0
    entries = jax.random.normal(stream_key, extent, jnp.float32) * scale * loudness
    return jnp.minimum(jnp.maximum(entries, -reach), reach).astype(held_as)


def setup_inputs(seed: int = 0, part: int = 0) -> dict:
    splits = jax.random.split(jax.random.key(seed), 4)
    part_keys = jax.random.split(jax.random.fold_in(splits[3], part), 4)
    subspace = normal_values(part_keys[0], (COLS, NZ, PLANE), 1.0, 6.0, ((1, 4),), jnp.float32)
    potential = jnp.clip(jax.random.uniform(part_keys[1], (NZ, PLANE), jnp.float32, -2.0, 2.0) * steps_of(part_keys[1], (NZ, PLANE), ((0, 4),), -0.4, 0.0), -2.0, 2.0)
    slow_shifts = draw_slow_shifts(jax.random.fold_in(jax.random.fold_in(splits[3], part), 71), part)
    return dict(subspace=subspace, potential=potential, slow_shifts=slow_shifts)


RADIUS = 4.0


def plane_sum(values_in):
    width = values_in.shape[-1]
    leading = values_in.shape[:-1]
    rows_zero = jnp.zeros(leading + (LY,), jnp.float32)
    one_zero = jnp.zeros(leading + (1,), jnp.float32)
    column = jnp.arange(width) % LY
    keep_next = (column != LY - 1).astype(jnp.float32)
    keep_prior = (column != 0).astype(jnp.float32)
    running = jnp.concatenate([values_in[..., LY:], rows_zero], -1) + jnp.concatenate([rows_zero, values_in[..., :-LY]], -1)
    running = running + jnp.concatenate([values_in[..., 1:], one_zero], -1) * keep_next
    running = running + jnp.concatenate([one_zero, values_in[..., :-1]], -1) * keep_prior
    return running


def combine(vector, neighbours, z_real, z_imag, potential):
    shift_re = z_real[:, None, None, None]
    shift_im = z_imag[:, None, None, None]
    real_part = vector[:, 0]
    imag_part = vector[:, 1]
    out_re = shift_re * real_part - shift_im * imag_part + neighbours[:, 0] - potential * real_part
    out_im = shift_re * imag_part + shift_im * real_part + neighbours[:, 1] - potential * imag_part
    return jnp.stack([out_re, out_im], 1)


def shifted_apply(vector, z_real, z_imag, potential):
    padded = jnp.pad(vector, ((0, 0), (0, 0), (0, 0), (1, 1), (0, 0)))
    neighbours = padded[:, :, :, 2:, :] + padded[:, :, :, :-2, :] + plane_sum(vector)
    return combine(vector, neighbours, z_real, z_imag, potential)


def cscale(num_re, num_im, vector):
    scale_re = num_re[:, :, None, None]
    scale_im = num_im[:, :, None, None]
    return jnp.stack([scale_re * vector[:, 0] - scale_im * vector[:, 1], scale_re * vector[:, 1] + scale_im * vector[:, 0]], 1)


def cdiv(top_re, top_im, low_re, low_im):
    magnitude = low_re * low_re + low_im * low_im
    return (top_re * low_re + top_im * low_im) / magnitude, (top_im * low_re - top_re * low_im) / magnitude


def cmul(left_re, left_im, right_re, right_im):
    return left_re * right_re - left_im * right_im, left_re * right_im + left_im * right_re


def project(source, vector):
    return jnp.sum(source * vector[:, 0], axis=(2, 3)), jnp.sum(source * vector[:, 1], axis=(2, 3))


def inner(left_vec, right_vec):
    real_sum = jnp.sum(left_vec[:, 0] * right_vec[:, 0] + left_vec[:, 1] * right_vec[:, 1], axis=(2, 3))
    imag_sum = jnp.sum(left_vec[:, 0] * right_vec[:, 1] - left_vec[:, 1] * right_vec[:, 0], axis=(2, 3))
    return real_sum, imag_sum


def step_once(carried, source, z_real, z_imag, potential, active):
    solution, residual, search, rho_re, rho_im = carried
    image = shifted_apply(search, z_real, z_imag, potential)
    den_re, den_im = project(source, image)
    alpha_re, alpha_im = cdiv(rho_re, rho_im, den_re, den_im)
    middle = residual - cscale(alpha_re, alpha_im, image)
    second = shifted_apply(middle, z_real, z_imag, potential)
    ts_re, ts_im = inner(second, middle)
    t_norm = jnp.sum(second * second, axis=(1, 3, 4))
    omega_re = ts_re / t_norm
    omega_im = ts_im / t_norm
    new_solution = solution + cscale(alpha_re, alpha_im, search) + cscale(omega_re, omega_im, middle)
    new_residual = middle - cscale(omega_re, omega_im, second)
    new_rho_re, new_rho_im = project(source, new_residual)
    ratio_re, ratio_im = cdiv(new_rho_re, new_rho_im, rho_re, rho_im)
    quot_re, quot_im = cdiv(alpha_re, alpha_im, omega_re, omega_im)
    beta_re, beta_im = cmul(ratio_re, ratio_im, quot_re, quot_im)
    new_search = new_residual + cscale(beta_re, beta_im, search - cscale(omega_re, omega_im, image))
    keep_vec = active[:, None, None, None, None]
    keep_sca = active[:, None]
    return (jnp.where(keep_vec, new_solution, solution), jnp.where(keep_vec, new_residual, residual),
            jnp.where(keep_vec, new_search, search), jnp.where(keep_sca, new_rho_re, rho_re),
            jnp.where(keep_sca, new_rho_im, rho_im))


def reference(subspace, potential, slow_shifts):
    source = subspace[None]

    def one_shift(running, shift_id):
        angles = (shift_id.astype(jnp.float32) + 0.5) * (math.pi / NS)
        z_real = jnp.reshape(RADIUS * jnp.cos(angles), (1,))
        z_imag = jnp.reshape(RADIUS * jnp.sin(angles), (1,))
        iter_count = jnp.where((shift_id == slow_shifts[0]) | (shift_id == slow_shifts[1]), SLOW, FAST)
        residual = jnp.stack([source, jnp.zeros_like(source)], 1)
        rho_re = jnp.sum(source * source, axis=(2, 3))
        carried = (jnp.zeros_like(residual), residual, residual, rho_re, jnp.zeros_like(rho_re))

        def advance(step_no, state):
            active = jnp.reshape(iter_count > step_no, (1,))
            return step_once(state, source, z_real, z_imag, potential, active)

        carried = lax.fori_loop(0, SLOW, advance, carried)
        solution = carried[0]
        weight_re = z_real[0] / NS
        weight_im = z_imag[0] / NS
        return running + (weight_re * solution[0, 0] - weight_im * solution[0, 1]), None

    running, _ = lax.scan(one_shift, jnp.zeros(subspace.shape, subspace.dtype), jnp.arange(NS, dtype=jnp.int32))
    return running
```

```python
import functools
import math

import jax
import jax.numpy as jnp
import numpy as np
from jax import lax
from jax.experimental import pallas as pl
from jax.experimental.pallas import tpu as pltpu
from jax.sharding import PartitionSpec as P

NS = 8
FAST = 2
SLOW = 4
LY = 32
RADIUS = 4.0
SPAN = 8.0
LANES = 128
ROWS = 8
DEGREE = 2 * SLOW
MOMENTS = 2 * DEGREE + 1
MESH = pl.DeviceIdType.MESH


def shift_constants():
    angles = (np.arange(NS, dtype=np.float32) + np.float32(0.5)) * np.float32(math.pi / NS)
    return (np.float32(RADIUS) * np.cos(angles), np.float32(RADIUS) * np.sin(angles))


def by_lane(lane, values):
    picked = jnp.full(lane.shape, float(values[0]), jnp.float32)
    for index in range(1, len(values)):
        picked = jnp.where(lane == index, float(values[index]), picked)
    return picked


def cdiv(top, low):
    magnitude = low[0] * low[0] + low[1] * low[1]
    return (
        (top[0] * low[0] + top[1] * low[1]) / magnitude,
        (top[1] * low[0] - top[0] * low[1]) / magnitude,
    )


def cmul(left, right):
    return (left[0] * right[0] - left[1] * right[1], left[0] * right[1] + left[1] * right[0])


def cadd(left, right):
    return (left[0] + right[0], left[1] + right[1])


def csub(left, right):
    return (left[0] - right[0], left[1] - right[1])


def times_h(poly):
    count = len(poly)
    out = []
    for j in range(count + 1):
        terms = []
        if j >= 1:
            weight = SPAN if j == 1 else SPAN / 2
            terms.append(tuple(weight * part for part in poly[j - 1]))
        if j + 1 < count:
            terms.append(tuple(SPAN / 2 * part for part in poly[j + 1]))
        if not terms:
            terms.append(tuple(jnp.zeros_like(part) for part in poly[0]))
        total = terms[0]
        for term in terms[1:]:
            total = cadd(total, term)
        out.append(total)
    return out


def shifted(poly, z):
    image = times_h(poly)
    return [cadd(image[j], cmul(z, poly[j])) if j < len(poly) else image[j] for j in range(len(image))]


def total_of(terms):
    terms = list(terms)
    while len(terms) > 1:
        terms = [
            terms[i] + terms[i + 1] if i + 1 < len(terms) else terms[i]
            for i in range(0, len(terms), 2)
        ]
    return terms[0]


def project(poly, moments):
    return tuple(total_of(poly[j][part] * moments[j] for j in range(len(poly))) for part in (0, 1))


def gram_times(gram, poly, count):
    return [
        tuple(total_of(gram[i][j] * poly[j][part] for j in range(len(poly))) for part in (0, 1))
        for i in range(count)
    ]


def solve(moments, z, slow):
    gram = [
        [0.5 * (moments[i + j] + moments[abs(i - j)]) for j in range(DEGREE + 1)]
        for i in range(DEGREE + 1)
    ]
    zero = jnp.zeros_like(moments[0])
    one = jnp.ones_like(moments[0])
    solution = [(zero, zero)] * DEGREE
    residual = [(one, zero)]
    search = [(one, zero)]
    rho = (moments[0], zero)
    for step in range(SLOW):
        image = shifted(search, z)
        alpha = cdiv(rho, project(image, moments))
        middle = [
            csub(residual[j], cmul(alpha, image[j])) if j < len(residual)
            else tuple(-part for part in cmul(alpha, image[j]))
            for j in range(len(image))
        ]
        second = shifted(middle, z)
        low = gram_times(gram, middle, len(second))
        high = gram_times(gram, second, len(second))
        pairs = list(zip(second, low, high))
        ts_re = total_of(s[0] * a[0] + s[1] * a[1] for s, a, _ in pairs)
        ts_im = total_of(s[0] * a[1] - s[1] * a[0] for s, a, _ in pairs)
        t_norm = total_of(s[0] * b[0] + s[1] * b[1] for s, _, b in pairs)
        omega = (ts_re / t_norm, ts_im / t_norm)
        for j in range(len(middle)):
            change = cmul(omega, middle[j])
            if j < len(search):
                change = cadd(change, cmul(alpha, search[j]))
            new = cadd(solution[j], change)
            if step >= FAST:
                new = tuple(jnp.where(slow, a, b) for a, b in zip(new, solution[j]))
            solution[j] = new
        if step == SLOW - 1:
            break
        residual = [
            csub(middle[j], cmul(omega, second[j])) if j < len(middle)
            else tuple(-part for part in cmul(omega, second[j]))
            for j in range(len(second))
        ]
        rho_new = project(residual, moments)
        beta = cmul(cdiv(rho_new, rho), cdiv(alpha, omega))
        rho = rho_new
        inner = [
            csub(search[j], cmul(omega, image[j])) if j < len(search)
            else tuple(-part for part in cmul(omega, image[j]))
            for j in range(len(image))
        ]
        search = [
            cadd(residual[j], cmul(beta, inner[j])) if j < len(inner) else residual[j]
            for j in range(len(residual))
        ]
    return solution


def neighbour_sum(groups, lane):
    depth = groups[0].shape[1]
    low = [pltpu.roll(v, LY, 2) for v in groups]
    high = [pltpu.roll(v, LANES - LY, 2) for v in groups]
    zero = jnp.zeros_like(groups[0])
    out = []
    for g, v in enumerate(groups):
        total = jnp.where(lane < LY, low[g - 1] if g else zero, low[g])
        after = high[g + 1] if g + 1 < len(groups) else zero
        total = total + jnp.where(lane >= LANES - LY, after, high[g])
        total = total + jnp.where(lane % LY == 0, 0.0, pltpu.roll(v, 1, 2))
        total = total + jnp.where(lane % LY == LY - 1, 0.0, pltpu.roll(v, LANES - 1, 2))
        total = total + pltpu.roll(v, 1, 1) + pltpu.roll(v, depth - 1, 1)
        out.append(total)
    return out


def kernel(count, sub_ref, pot_ref, slow_ref, out_ref, field, disorder, parts,
           own_sem, send_sem, recv_sem, part_send, part_recv):
    me = lax.axis_index("slab")
    cols, planes, cells = out_ref.shape
    group_count = cells // LANES
    mine = sub_ref.at[pl.ds(lax.axis_index("shift") * cols, cols)]

    own = [
        pltpu.make_async_copy(mine, field.at[1], own_sem.at[0]),
        pltpu.make_async_copy(pot_ref, disorder.at[1], own_sem.at[1]),
    ]
    for copy in own:
        copy.start()

    barrier = pltpu.get_barrier_semaphore()
    for offset in range(1, count):
        pl.semaphore_signal(
            barrier, inc=1, device_id={"slab": lax.rem(me + offset, count)}, device_id_type=MESH
        )
    pl.semaphore_wait(barrier, count - 1)

    def halo(side):
        target = me + 1 if side == 0 else me - 1
        return [
            pltpu.make_async_remote_copy(
                src_ref=source, dst_ref=place, send_sem=send_sem.at[side, which],
                recv_sem=recv_sem.at[side, which], device_id={"slab": target}, device_id_type=MESH,
            )
            for which, (source, place) in enumerate(
                ((mine, field.at[2 * side]), (pot_ref, disorder.at[2 * side]))
            )
        ]

    has_low, has_high = me > 0, me < count - 1

    @pl.when(has_high)
    def _():
        for copy in halo(0):
            copy.start()

    @pl.when(has_low)
    def _():
        for copy in halo(1):
            copy.start()

    @pl.when(jnp.logical_not(has_low))
    def _():
        field[0] = jnp.zeros((cols, planes, cells), jnp.float32)
        disorder[0] = jnp.zeros((planes, cells), jnp.float32)

    @pl.when(jnp.logical_not(has_high))
    def _():
        field[2] = jnp.zeros((cols, planes, cells), jnp.float32)
        disorder[2] = jnp.zeros((planes, cells), jnp.float32)

    for copy in own:
        copy.wait()

    @pl.when(has_low)
    def _():
        for copy in halo(0):
            copy.wait_recv()

    @pl.when(has_high)
    def _():
        for copy in halo(1):
            copy.wait_recv()

    depth = 3 * planes
    lane = lax.broadcasted_iota(jnp.int32, (1, 1, LANES), 2)
    plane = lax.broadcasted_iota(jnp.int32, (1, depth, LANES), 1)
    inside = jnp.where(has_low, 1, 0) * planes, jnp.where(has_high, 2, 1) * planes
    gain = jnp.where(
        (plane >= planes - inside[0]) & (plane < planes + inside[1]), 2.0 / SPAN, 0.0
    )
    spans = [slice(g * LANES, (g + 1) * LANES) for g in range(group_count)]
    potential = [
        jnp.concatenate([disorder[i, :, s] for i in range(3)], 0)[None] * gain for s in spans
    ]
    before = None
    current = [jnp.concatenate([field[i, :, :, s] for i in range(3)], 1) for s in spans]
    basis = [[v[:, planes:2 * planes] for v in current]]
    for step in range(DEGREE):
        image = [
            gain * total - pot * v
            for total, pot, v in zip(neighbour_sum(current, lane), potential, current)
        ]
        if step == 0:
            following = [0.5 * v for v in image]
        else:
            following = [v - old for v, old in zip(image, before)]
        before, current = current, following
        basis.append([v[:, planes:2 * planes] for v in current])

    lane_of = lax.broadcasted_iota(jnp.int32, (ROWS, LANES), 1)
    payload = jnp.zeros((ROWS, LANES), jnp.float32)
    for k in range(MOMENTS):
        left, right = basis[k // 2], basis[(k + 1) // 2]
        product = total_of(a * b for a, b in zip(left, right))
        rows = jnp.sum(product, axis=1)
        if cols < ROWS:
            rows = jnp.concatenate([rows, jnp.ones((ROWS - cols, LANES), jnp.float32)], 0)
        payload = jnp.where(lane_of == k, jnp.sum(rows, axis=1, keepdims=True), payload)
    parts[me] = payload

    def part(offset):
        return pltpu.make_async_remote_copy(
            src_ref=parts.at[me], dst_ref=parts.at[me], send_sem=part_send.at[offset - 1],
            recv_sem=part_recv.at[offset - 1], device_id={"slab": lax.rem(me + offset, count)},
            device_id_type=MESH,
        )

    for offset in range(1, count):
        part(offset).start()

    z_values = shift_constants()
    z = (by_lane(lane_of, z_values[0]), by_lane(lane_of, z_values[1]))
    slow = (lane_of == slow_ref[0]) | (lane_of == slow_ref[1])

    for offset in range(1, count):
        part(offset).wait_recv()
    whole = total_of(parts[index] for index in range(count))
    sums = [jnp.broadcast_to(whole[:, k:k + 1], (ROWS, LANES)) for k in range(MOMENTS)]
    moments = [sums[0], sums[1]]
    for k in range(2, MOMENTS):
        moments.append(2.0 * sums[k] - sums[k % 2])
    solution_of = solve(moments, z, slow)
    weight = (z[0] / NS, z[1] / NS)
    scales = []
    for re_part, im_part in solution_of:
        value = jnp.where(lane_of < NS, weight[0] * re_part - weight[1] * im_part, 0.0)
        scales.append(jnp.sum(value, axis=1, keepdims=True)[:cols].reshape(cols, 1, 1))
    for g, s in enumerate(spans):
        out_ref[:, :, s] = total_of(scale * v[g] for scale, v in zip(scales, basis))

    for offset in range(1, count):
        part(offset).wait_send()

    @pl.when(has_high)
    def _():
        for copy in halo(0):
            copy.wait_send()

    @pl.when(has_low)
    def _():
        for copy in halo(1):
            copy.wait_send()


def local(subspace, potential, slow_shifts):
    columns, planes, cells = subspace.shape
    count = lax.axis_size("slab")
    cols = columns // lax.axis_size("shift")
    links = max(count - 1, 1)
    return pl.pallas_call(
        functools.partial(kernel, count),
        out_shape=jax.ShapeDtypeStruct((cols, planes, cells), jnp.float32),
        in_specs=[
            pl.BlockSpec(memory_space=pl.ANY),
            pl.BlockSpec(memory_space=pl.ANY),
            pl.BlockSpec(memory_space=pltpu.SMEM),
        ],
        out_specs=pl.BlockSpec(memory_space=pltpu.VMEM),
        scratch_shapes=[
            pltpu.VMEM((3, cols, planes, cells), jnp.float32),
            pltpu.VMEM((3, planes, cells), jnp.float32),
            pltpu.VMEM((count, ROWS, LANES), jnp.float32),
            pltpu.SemaphoreType.DMA((2,)),
            pltpu.SemaphoreType.DMA((2, 2)),
            pltpu.SemaphoreType.DMA((2, 2)),
            pltpu.SemaphoreType.DMA((links,)),
            pltpu.SemaphoreType.DMA((links,)),
        ],
        compiler_params=pltpu.CompilerParams(collective_id=0, has_side_effects=True),
    )(subspace, potential, slow_shifts)


def solution(mesh):
    return jax.shard_map(
        local,
        mesh=mesh,
        in_specs=(P(None, ("dom", "slab"), None), P(("dom", "slab"), None), P("dom")),
        out_specs=P("shift", ("dom", "slab"), None),
        check_vma=False,
    )
```

```python
import functools
import math

import jax
import jax.numpy as jnp
import numpy as np
from jax import lax
from jax.experimental import pallas as pl
from jax.experimental.pallas import tpu as pltpu
from jax.sharding import PartitionSpec as P

NS = 8
FAST = 2
SLOW = 4
LY = 32
RADIUS = 4.0
SCALE = 4.0
LANES = 128
DEGREE = 2 * SLOW
MESH = pl.DeviceIdType.MESH


def shift_constants():
    angles = (np.arange(NS, dtype=np.float32) + np.float32(0.5)) * np.float32(math.pi / NS)
    return (np.float32(RADIUS) * np.cos(angles), np.float32(RADIUS) * np.sin(angles))


def by_lane(lane, values):
    picked = jnp.full(lane.shape, float(values[0]), jnp.float32)
    for index in range(1, len(values)):
        picked = jnp.where(lane == index, float(values[index]), picked)
    return picked


def cdiv(top, low):
    magnitude = low[0] * low[0] + low[1] * low[1]
    return (
        (top[0] * low[0] + top[1] * low[1]) / magnitude,
        (top[1] * low[0] - top[0] * low[1]) / magnitude,
    )


def cmul(left, right):
    return (left[0] * right[0] - left[1] * right[1], left[0] * right[1] + left[1] * right[0])


def cadd(left, right):
    return (left[0] + right[0], left[1] + right[1])


def csub(left, right):
    return (left[0] - right[0], left[1] - right[1])


def total_of(terms):
    terms = list(terms)
    while len(terms) > 1:
        terms = [
            terms[i] + terms[i + 1] if i + 1 < len(terms) else terms[i]
            for i in range(0, len(terms), 2)
        ]
    return terms[0]


def shifted(poly, z, diagonal, upper):
    count = len(poly)
    out = []
    for j in range(count + 1):
        terms = []
        if j < count:
            terms.append(cmul((z[0] + diagonal[j], z[1]), poly[j]))
        if j >= 1:
            terms.append(tuple(SCALE * part for part in poly[j - 1]))
        if j + 1 < count:
            terms.append(tuple(upper[j + 1] * part for part in poly[j + 1]))
        out.append(tuple(total_of(term[part] for term in terms) for part in (0, 1)))
    return out


def minus(left, factor, right):
    out = []
    for j, value in enumerate(right):
        change = cmul(factor, value)
        out.append(csub(left[j], change) if j < len(left) else (-change[0], -change[1]))
    return out


def solve(norms, diagonal, upper, z, slow):
    zero = jnp.zeros_like(z[0])
    one = jnp.ones_like(z[0])
    solution = [(zero, zero)] * DEGREE
    residual = [(one, zero)]
    search = [(one, zero)]
    for step in range(SLOW):
        image = shifted(search, z, diagonal, upper)
        alpha = cdiv(residual[0], image[0])
        middle = minus(residual, alpha, image)
        second = shifted(middle, z, diagonal, upper)
        heavy = [tuple(norms[j] * part for part in second[j]) for j in range(len(second))]
        pairs = list(zip(heavy, middle))
        ts_re = total_of(s[0] * m[0] + s[1] * m[1] for s, m in pairs)
        ts_im = total_of(s[0] * m[1] - s[1] * m[0] for s, m in pairs)
        t_norm = total_of(h[0] * s[0] + h[1] * s[1] for h, s in zip(heavy, second))
        omega = (ts_re / t_norm, ts_im / t_norm)
        for j in range(len(middle)):
            change = cmul(omega, middle[j])
            if j < len(search):
                change = cadd(change, cmul(alpha, search[j]))
            new = cadd(solution[j], change)
            if step >= FAST:
                new = tuple(jnp.where(slow, a, b) for a, b in zip(new, solution[j]))
            solution[j] = new
        if step == SLOW - 1:
            break
        before = residual[0]
        residual = minus(middle, omega, second)
        beta = cmul(cdiv(residual[0], before), cdiv(alpha, omega))
        inner = minus(search, omega, image)
        search = [
            cadd(residual[j], cmul(beta, inner[j])) if j < len(inner) else residual[j]
            for j in range(len(residual))
        ]
    return solution


def neighbour_sum(groups, lane, row):
    depth = groups[0].shape[0]
    low = [pltpu.roll(v, LY, 1) for v in groups]
    high = [pltpu.roll(v, LANES - LY, 1) for v in groups]
    zero = jnp.zeros_like(groups[0])
    out = []
    for g, v in enumerate(groups):
        after = high[g + 1] if g + 1 < len(groups) else zero
        out.append(total_of([
            jnp.where(lane < LY, low[g - 1] if g else zero, low[g]),
            jnp.where(lane >= LANES - LY, after, high[g]),
            jnp.where(lane % LY == 0, 0.0, pltpu.roll(v, 1, 1)),
            jnp.where(lane % LY == LY - 1, 0.0, pltpu.roll(v, LANES - 1, 1)),
            jnp.where(row == 0, 0.0, pltpu.roll(v, 1, 0)),
            jnp.where(row == depth - 1, 0.0, pltpu.roll(v, depth - 1, 0)),
        ]))
    return out


def dot(left, right):
    product = total_of(a * b for a, b in zip(left, right))
    return jnp.sum(jnp.sum(product, axis=0, keepdims=True), axis=1, keepdims=True)


def filtered_column(groups, potential, slow_first, slow_second):
    depth = groups[0].shape[0]
    lane = lax.broadcasted_iota(jnp.int32, (1, LANES), 1)
    field_lane = lax.broadcasted_iota(jnp.int32, (depth, LANES), 1)
    field_row = lax.broadcasted_iota(jnp.int32, (depth, LANES), 0)
    potential = [v * (1.0 / SCALE) for v in potential]
    basis = [groups]
    norms, diagonal, upper = [dot(groups, groups)], [], [None]
    for step in range(DEGREE):
        current = basis[-1]
        norm = norms[-1]
        inverse = jnp.where(norm > 0.0, 1.0 / norm, 0.0)
        image = [
            total * (1.0 / SCALE) - pot * v
            for total, pot, v in zip(neighbour_sum(current, field_lane, field_row), potential, current)
        ]
        if step:
            image = [v - ratio * old for v, old in zip(image, basis[-2])]
        shift = dot(current, image) * inverse
        following = [v - shift * old for v, old in zip(image, current)]
        basis.append(following)
        norms.append(dot(following, following))
        ratio = norms[-1] * inverse
        diagonal.append(SCALE * shift)
        upper.append(SCALE * ratio)
    z_values = shift_constants()
    z = (by_lane(lane, z_values[0]), by_lane(lane, z_values[1]))
    slow = (lane == slow_first) | (lane == slow_second)
    solution_of = solve(norms, diagonal, upper, z, slow)
    weight = (z[0] / NS, z[1] / NS)
    scales = [
        jnp.sum(
            jnp.where(lane < NS, weight[0] * re_part - weight[1] * im_part, 0.0),
            axis=1, keepdims=True,
        )
        for re_part, im_part in solution_of
    ]
    return [
        total_of(scale * v[g] for scale, v in zip(scales, basis)) for g in range(len(groups))
    ]


def kernel(count, cols, sub_ref, pot_ref, slow_ref, out_ref, field, disorder, result,
           own_sem, send_sem, recv_sem, back_send, back_recv):
    me = lax.axis_index("slab")
    planes, cells = pot_ref.shape
    stride = count // cols
    first = lax.axis_index("shift") * cols
    mine = me // stride
    owner = me % stride == 0

    def when_owner(body):
        if stride == 1:
            body()
        else:
            pl.when(owner)(body)

    def outwards(hop):
        column = lax.rem(mine + hop, cols)
        return [
            pltpu.make_async_remote_copy(
                src_ref=source, dst_ref=place.at[me], send_sem=send_sem.at[hop, which],
                recv_sem=recv_sem.at[me, which], device_id={"slab": column * stride},
                device_id_type=MESH,
            )
            for which, (source, place) in enumerate(
                ((sub_ref.at[first + column], field), (pot_ref, disorder))
            )
        ]

    def inwards(offset):
        source = lax.rem(me + offset, count)
        return [
            pltpu.make_async_remote_copy(
                src_ref=place.at[source], dst_ref=place.at[source], send_sem=send_sem.at[0, which],
                recv_sem=recv_sem.at[source, which], device_id={"slab": source},
                device_id_type=MESH,
            )
            for which, place in enumerate((field, disorder))
        ]

    def home(offset):
        target = lax.rem(me + offset, count)
        return pltpu.make_async_remote_copy(
            src_ref=result.at[target], dst_ref=out_ref.at[mine], send_sem=back_send.at[offset],
            recv_sem=back_recv.at[mine], device_id={"slab": target}, device_id_type=MESH,
        )

    def arriving(hop):
        column = lax.rem(mine + hop, cols)
        return pltpu.make_async_remote_copy(
            src_ref=result.at[0], dst_ref=out_ref.at[column], send_sem=back_send.at[0],
            recv_sem=back_recv.at[column], device_id={"slab": column * stride},
            device_id_type=MESH,
        )

    own = [
        pltpu.make_async_copy(sub_ref.at[first + mine], field.at[me], own_sem.at[0]),
        pltpu.make_async_copy(pot_ref, disorder.at[me], own_sem.at[1]),
    ]

    @when_owner
    def _():
        for copy in own:
            copy.start()

    barrier = pltpu.get_barrier_semaphore()
    for offset in range(1, count):
        pl.semaphore_signal(
            barrier, inc=1, device_id={"slab": lax.rem(me + offset, count)}, device_id_type=MESH
        )
    pl.semaphore_wait(barrier, count - 1)

    if stride > 1:
        @pl.when(jnp.logical_not(owner))
        def _():
            for copy in outwards(0):
                copy.start()

    for hop in range(1, cols):
        for copy in outwards(hop):
            copy.start()

    @when_owner
    def _():
        for copy in own:
            copy.wait()
        for offset in range(1, count):
            for copy in inwards(offset):
                copy.wait_recv()
        spans = [slice(g, g + LANES) for g in range(0, cells, LANES)]
        groups = [field[:, :, s].reshape(count * planes, LANES) for s in spans]
        potential = [disorder[:, :, s].reshape(count * planes, LANES) for s in spans]
        answer = filtered_column(groups, potential, slow_ref[0], slow_ref[1])
        for s, value in zip(spans, answer):
            result[:, :, s] = value.reshape(count, planes, LANES)
        keep = pltpu.make_async_copy(result.at[me], out_ref.at[mine], own_sem.at[0])
        keep.start()
        for offset in range(1, count):
            home(offset).start()
        keep.wait()
        for offset in range(1, count):
            home(offset).wait_send()

    if stride > 1:
        @pl.when(jnp.logical_not(owner))
        def _():
            arriving(0).wait_recv()
            for copy in outwards(0):
                copy.wait_send()

    for hop in range(1, cols):
        arriving(hop).wait_recv()
        for copy in outwards(hop):
            copy.wait_send()


def local(subspace, potential, slow_shifts):
    columns, planes, cells = subspace.shape
    count = lax.axis_size("slab")
    cols = columns // lax.axis_size("shift")
    return pl.pallas_call(
        functools.partial(kernel, count, cols),
        out_shape=jax.ShapeDtypeStruct((cols, planes, cells), jnp.float32),
        in_specs=[
            pl.BlockSpec(memory_space=pl.ANY),
            pl.BlockSpec(memory_space=pl.ANY),
            pl.BlockSpec(memory_space=pltpu.SMEM),
        ],
        out_specs=pl.BlockSpec(memory_space=pl.ANY),
        scratch_shapes=[
            pltpu.VMEM((count, planes, cells), jnp.float32),
            pltpu.VMEM((count, planes, cells), jnp.float32),
            pltpu.VMEM((count, planes, cells), jnp.float32),
            pltpu.SemaphoreType.DMA((2,)),
            pltpu.SemaphoreType.DMA((cols, 2)),
            pltpu.SemaphoreType.DMA((count, 2)),
            pltpu.SemaphoreType.DMA((count,)),
            pltpu.SemaphoreType.DMA((cols,)),
        ],
        compiler_params=pltpu.CompilerParams(collective_id=0, has_side_effects=True),
    )(subspace, potential, slow_shifts)


def solution(mesh):
    return jax.shard_map(
        local,
        mesh=mesh,
        in_specs=(P(None, ("dom", "slab"), None), P(("dom", "slab"), None), P("dom")),
        out_specs=P("shift", ("dom", "slab"), None),
        check_vma=False,
    )
```

```python
import functools
import math

import jax
import jax.numpy as jnp
import numpy as np
from jax import lax
from jax.experimental import pallas as pl
from jax.experimental.pallas import tpu as pltpu
from jax.sharding import PartitionSpec as P

NS = 8
FAST = 2
SLOW = 4
LY = 32
RADIUS = 4.0
SCALE = 4.0
LANES = 128
DEGREE = 2 * SLOW
PIECES = 2
MESH = pl.DeviceIdType.MESH


def shift_constants():
    angles = (np.arange(NS, dtype=np.float32) + np.float32(0.5)) * np.float32(math.pi / NS)
    return (np.float32(RADIUS) * np.cos(angles), np.float32(RADIUS) * np.sin(angles))


def by_lane(lane, values):
    picked = jnp.full(lane.shape, float(values[0]), jnp.float32)
    for index in range(1, len(values)):
        picked = jnp.where(lane == index, float(values[index]), picked)
    return picked


def cdiv(top, low):
    magnitude = low[0] * low[0] + low[1] * low[1]
    return (
        (top[0] * low[0] + top[1] * low[1]) / magnitude,
        (top[1] * low[0] - top[0] * low[1]) / magnitude,
    )


def cmul(left, right):
    return (left[0] * right[0] - left[1] * right[1], left[0] * right[1] + left[1] * right[0])


def cadd(left, right):
    return (left[0] + right[0], left[1] + right[1])


def csub(left, right):
    return (left[0] - right[0], left[1] - right[1])


def total_of(terms):
    terms = list(terms)
    while len(terms) > 1:
        terms = [
            terms[i] + terms[i + 1] if i + 1 < len(terms) else terms[i]
            for i in range(0, len(terms), 2)
        ]
    return terms[0]


def shifted(poly, z, diagonal, upper):
    count = len(poly)
    out = []
    for j in range(count + 1):
        terms = []
        if j < count:
            terms.append(cmul((z[0] + diagonal[j], z[1]), poly[j]))
        if j >= 1:
            terms.append(tuple(SCALE * part for part in poly[j - 1]))
        if j + 1 < count:
            terms.append(tuple(upper[j + 1] * part for part in poly[j + 1]))
        out.append(tuple(total_of(term[part] for term in terms) for part in (0, 1)))
    return out


def minus(left, factor, right):
    out = []
    for j, value in enumerate(right):
        change = cmul(factor, value)
        out.append(csub(left[j], change) if j < len(left) else (-change[0], -change[1]))
    return out


def solve(norms, diagonal, upper, z, slow):
    zero = jnp.zeros_like(z[0])
    one = jnp.ones_like(z[0])
    solution = [(zero, zero)] * DEGREE
    residual = [(one, zero)]
    search = [(one, zero)]
    for step in range(SLOW):
        image = shifted(search, z, diagonal, upper)
        alpha = cdiv(residual[0], image[0])
        middle = minus(residual, alpha, image)
        second = shifted(middle, z, diagonal, upper)
        heavy = [tuple(norms[j] * part for part in second[j]) for j in range(len(second))]
        pairs = list(zip(heavy, middle))
        ts_re = total_of(s[0] * m[0] + s[1] * m[1] for s, m in pairs)
        ts_im = total_of(s[0] * m[1] - s[1] * m[0] for s, m in pairs)
        t_norm = total_of(h[0] * s[0] + h[1] * s[1] for h, s in zip(heavy, second))
        omega = (ts_re / t_norm, ts_im / t_norm)
        for j in range(len(middle)):
            change = cmul(omega, middle[j])
            if j < len(search):
                change = cadd(change, cmul(alpha, search[j]))
            new = cadd(solution[j], change)
            if step >= FAST:
                new = tuple(jnp.where(slow, a, b) for a, b in zip(new, solution[j]))
            solution[j] = new
        if step == SLOW - 1:
            break
        before = residual[0]
        residual = minus(middle, omega, second)
        beta = cmul(cdiv(residual[0], before), cdiv(alpha, omega))
        inner = minus(search, omega, image)
        search = [
            cadd(residual[j], cmul(beta, inner[j])) if j < len(inner) else residual[j]
            for j in range(len(residual))
        ]
    return solution


def neighbour_sum(groups, lane, row):
    depth = groups[0].shape[1]
    low = [pltpu.roll(v, LY, 2) for v in groups]
    high = [pltpu.roll(v, LANES - LY, 2) for v in groups]
    zero = jnp.zeros_like(groups[0])
    out = []
    for g, v in enumerate(groups):
        after = high[g + 1] if g + 1 < len(groups) else zero
        out.append(total_of([
            jnp.where(lane < LY, low[g - 1] if g else zero, low[g]),
            jnp.where(lane >= LANES - LY, after, high[g]),
            jnp.where(lane % LY == 0, 0.0, pltpu.roll(v, 1, 2)),
            jnp.where(lane % LY == LY - 1, 0.0, pltpu.roll(v, LANES - 1, 2)),
            jnp.where(row == 0, 0.0, pltpu.roll(v, 1, 1)),
            jnp.where(row == depth - 1, 0.0, pltpu.roll(v, depth - 1, 1)),
        ]))
    return out


def dot(left, right):
    product = total_of(a * b for a, b in zip(left, right))
    return jnp.sum(jnp.sum(product, axis=1, keepdims=True), axis=2, keepdims=True)


def column_scales(groups, potential, slow_first, slow_second):
    cols, depth = groups[0].shape[:2]
    field_lane = lax.broadcasted_iota(jnp.int32, (1, depth, LANES), 2)
    field_row = lax.broadcasted_iota(jnp.int32, (1, depth, LANES), 1)
    potential = [v[None] * (1.0 / SCALE) for v in potential]
    basis = [groups]
    norms, diagonal, upper = [dot(groups, groups)], [], [None]
    for step in range(DEGREE):
        current = basis[-1]
        norm = norms[-1]
        inverse = jnp.where(norm > 0.0, 1.0 / norm, 0.0)
        image = [
            total * (1.0 / SCALE) - pot * v
            for total, pot, v in zip(neighbour_sum(current, field_lane, field_row), potential, current)
        ]
        if step:
            image = [v - ratio * old for v, old in zip(image, basis[-2])]
        shift = dot(current, image) * inverse
        following = [v - shift * old for v, old in zip(image, current)]
        basis.append(following)
        norms.append(dot(following, following))
        ratio = norms[-1] * inverse
        diagonal.append(SCALE * shift)
        upper.append(SCALE * ratio)
    norms, diagonal, upper = (
        [None if v is None else v.reshape(cols, 1) for v in values]
        for values in (norms, diagonal, upper)
    )
    lane = lax.broadcasted_iota(jnp.int32, (cols, LANES), 1)
    z_values = shift_constants()
    z = (by_lane(lane, z_values[0]), by_lane(lane, z_values[1]))
    slow = (lane == slow_first) | (lane == slow_second)
    solution_of = solve(norms, diagonal, upper, z, slow)
    weight = (z[0] / NS, z[1] / NS)
    scales = [
        jnp.sum(
            jnp.where(lane < NS, weight[0] * re_part - weight[1] * im_part, 0.0),
            axis=1, keepdims=True,
        ).reshape(cols, 1, 1)
        for re_part, im_part in solution_of
    ]
    return basis, scales


def kernel(count, cols, chunk, sub_ref, pot_ref, slow_ref, out_ref, field, disorder, basis_ref,
           own_sem, send_sem, recv_sem):
    me = lax.axis_index("slab")
    planes, cells = pot_ref.shape
    mine = sub_ref.at[pl.ds(lax.axis_index("shift") * cols, cols)]
    has_low, has_high = me > 0, me < count - 1

    own = [
        pltpu.make_async_copy(pot_ref, disorder.at[me], own_sem.at[0]),
        pltpu.make_async_copy(mine, field.at[me], own_sem.at[1]),
    ]
    for copy in own:
        copy.start()

    barrier = pltpu.get_barrier_semaphore()

    @pl.when(has_low)
    def _():
        pl.semaphore_signal(barrier, inc=1, device_id={"slab": me - 1}, device_id_type=MESH)

    @pl.when(has_high)
    def _():
        pl.semaphore_signal(barrier, inc=1, device_id={"slab": me + 1}, device_id_type=MESH)

    pl.semaphore_wait(barrier, jnp.where(has_low, 1, 0) + jnp.where(has_high, 1, 0))

    half = cols // PIECES

    def passing(slab, side, piece, fresh=False):
        if piece == 0:
            place = disorder.at[slab]
            source = pot_ref if fresh else place
        else:
            rows = pl.ds((piece - 1) * half, half)
            place = field.at[slab, rows]
            source = mine.at[rows] if fresh else place
        return pltpu.make_async_remote_copy(
            src_ref=source, dst_ref=place, send_sem=send_sem.at[side, slab, piece],
            recv_sem=recv_sem.at[slab, piece],
            device_id={"slab": me + 1 if side == 0 else me - 1}, device_id_type=MESH,
        )

    pieces = range(PIECES + 1)
    for piece in pieces:
        @pl.when(has_high)
        def _():
            passing(me, 0, piece, True).start()

        @pl.when(has_low)
        def _():
            passing(me, 1, piece, True).start()

    def relay(hop):
        for piece in pieces:
            @pl.when(me >= hop)
            def _():
                passing(me - hop, 0, piece).wait_recv()

                @pl.when(has_high)
                def _():
                    passing(me - hop, 0, piece).start()

            @pl.when(me + hop < count)
            def _():
                passing(me + hop, 1, piece).wait_recv()

                @pl.when(has_low)
                def _():
                    passing(me + hop, 1, piece).start()

    def drain(hop):
        for piece in pieces:
            @pl.when((me >= hop) & has_high)
            def _():
                passing(me - hop, 0, piece).wait_send()

            @pl.when((me + hop < count) & has_low)
            def _():
                passing(me + hop, 1, piece).wait_send()

    def each_hop(first, body):
        if count <= 8:
            for hop in range(first, count):
                body(hop)
        else:
            lax.fori_loop(first, count, lambda hop, none: (body(hop), none)[1], 0)

    each_hop(1, relay)
    for copy in own:
        copy.wait()

    spans = [slice(g, g + LANES) for g in range(0, cells, LANES)]
    potential = [disorder[:, :, s].reshape(count * planes, LANES) for s in spans]

    def columns_from(start):
        rows = pl.ds(start, chunk)
        groups = [
            jnp.stack([field[:, start + c, :, s].reshape(count * planes, LANES) for c in range(chunk)])
            for s in spans
        ]
        basis, scales = column_scales(groups, potential, slow_ref[0], slow_ref[1])
        for j in range(DEGREE):
            for g, s in enumerate(spans):
                basis_ref[j, :, :, :, s] = basis[j][g].reshape(chunk, count, planes, LANES)
        for s in spans:
            out_ref[rows, :, s] = total_of(
                scale * basis_ref[j, :, me, :, s] for j, scale in enumerate(scales)
            )

    if chunk == cols:
        columns_from(0)
    else:
        lax.fori_loop(
            0, cols // chunk, lambda index, none: (columns_from(index * chunk), none)[1], 0
        )

    each_hop(0, drain)


def local(subspace, potential, slow_shifts):
    columns, planes, cells = subspace.shape
    count = lax.axis_size("slab")
    cols = columns // lax.axis_size("shift")
    chunk = cols if count * planes <= 64 else 1
    return pl.pallas_call(
        functools.partial(kernel, count, cols, chunk),
        out_shape=pltpu.VMEM((cols, planes, cells), jnp.float32),
        in_specs=[
            pl.BlockSpec(memory_space=pl.ANY),
            pl.BlockSpec(memory_space=pl.ANY),
            pl.BlockSpec(memory_space=pltpu.SMEM),
        ],
        out_specs=pl.BlockSpec(memory_space=pltpu.VMEM),
        scratch_shapes=[
            pltpu.VMEM((count, cols, planes, cells), jnp.float32),
            pltpu.VMEM((count, planes, cells), jnp.float32),
            pltpu.VMEM((DEGREE, chunk, count, planes, cells), jnp.float32),
            pltpu.SemaphoreType.DMA((2,)),
            pltpu.SemaphoreType.DMA((2, count, PIECES + 1)),
            pltpu.SemaphoreType.DMA((count, PIECES + 1)),
        ],
        compiler_params=pltpu.CompilerParams(
            collective_id=0, has_side_effects=True, vmem_limit_bytes=40 * 1024 * 1024
        ),
    )(subspace, potential, slow_shifts)


def solution(mesh):
    return jax.shard_map(
        local,
        mesh=mesh,
        in_specs=(P(None, ("dom", "slab"), None), P(("dom", "slab"), None), P("dom")),
        out_specs=P("shift", ("dom", "slab"), None),
        check_vma=False,
    )
```

```python
import functools
import math

import jax
import jax.numpy as jnp
import numpy as np
from jax import lax
from jax.experimental import pallas as pl
from jax.experimental.pallas import tpu as pltpu
from jax.sharding import PartitionSpec as P

NS = 8
FAST = 2
SLOW = 4
LY = 32
RADIUS = 4.0
SCALE = 4.0
LANES = 128
DEGREE = 2 * SLOW
MESH = pl.DeviceIdType.MESH


def shift_constants():
    angles = (np.arange(NS, dtype=np.float32) + np.float32(0.5)) * np.float32(math.pi / NS)
    return (np.float32(RADIUS) * np.cos(angles), np.float32(RADIUS) * np.sin(angles))


def by_lane(lane, values):
    picked = jnp.full(lane.shape, float(values[0]), jnp.float32)
    for index in range(1, len(values)):
        picked = jnp.where(lane == index, float(values[index]), picked)
    return picked


def cdiv(top, low):
    magnitude = low[0] * low[0] + low[1] * low[1]
    return (
        (top[0] * low[0] + top[1] * low[1]) / magnitude,
        (top[1] * low[0] - top[0] * low[1]) / magnitude,
    )


def cmul(left, right):
    return (left[0] * right[0] - left[1] * right[1], left[0] * right[1] + left[1] * right[0])


def cadd(left, right):
    return (left[0] + right[0], left[1] + right[1])


def csub(left, right):
    return (left[0] - right[0], left[1] - right[1])


def total_of(terms):
    terms = list(terms)
    while len(terms) > 1:
        terms = [
            terms[i] + terms[i + 1] if i + 1 < len(terms) else terms[i]
            for i in range(0, len(terms), 2)
        ]
    return terms[0]


def shifted(poly, z, diagonal, upper):
    count = len(poly)
    out = []
    for j in range(count + 1):
        terms = []
        if j < count:
            terms.append(cmul((z[0] + diagonal[j], z[1]), poly[j]))
        if j >= 1:
            terms.append(tuple(SCALE * part for part in poly[j - 1]))
        if j + 1 < count:
            terms.append(tuple(upper[j + 1] * part for part in poly[j + 1]))
        out.append(tuple(total_of(term[part] for term in terms) for part in (0, 1)))
    return out


def minus(left, factor, right):
    out = []
    for j, value in enumerate(right):
        change = cmul(factor, value)
        out.append(csub(left[j], change) if j < len(left) else (-change[0], -change[1]))
    return out


def solve(norms, diagonal, upper, z, slow):
    zero = jnp.zeros_like(z[0])
    one = jnp.ones_like(z[0])
    solution = [(zero, zero)] * DEGREE
    residual = [(one, zero)]
    search = [(one, zero)]
    for step in range(SLOW):
        image = shifted(search, z, diagonal, upper)
        alpha = cdiv(residual[0], image[0])
        middle = minus(residual, alpha, image)
        second = shifted(middle, z, diagonal, upper)
        heavy = [tuple(norms[j] * part for part in second[j]) for j in range(len(second))]
        pairs = list(zip(heavy, middle))
        ts_re = total_of(s[0] * m[0] + s[1] * m[1] for s, m in pairs)
        ts_im = total_of(s[0] * m[1] - s[1] * m[0] for s, m in pairs)
        t_norm = total_of(h[0] * s[0] + h[1] * s[1] for h, s in zip(heavy, second))
        omega = (ts_re / t_norm, ts_im / t_norm)
        for j in range(len(middle)):
            change = cmul(omega, middle[j])
            if j < len(search):
                change = cadd(change, cmul(alpha, search[j]))
            new = cadd(solution[j], change)
            if step >= FAST:
                new = tuple(jnp.where(slow, a, b) for a, b in zip(new, solution[j]))
            solution[j] = new
        if step == SLOW - 1:
            break
        before = residual[0]
        residual = minus(middle, omega, second)
        beta = cmul(cdiv(residual[0], before), cdiv(alpha, omega))
        inner = minus(search, omega, image)
        search = [
            cadd(residual[j], cmul(beta, inner[j])) if j < len(inner) else residual[j]
            for j in range(len(residual))
        ]
    return solution


def neighbour_sum(groups, lane, row):
    depth = groups[0].shape[0]
    low = [pltpu.roll(v, LY, 1) for v in groups]
    high = [pltpu.roll(v, LANES - LY, 1) for v in groups]
    zero = jnp.zeros_like(groups[0])
    out = []
    for g, v in enumerate(groups):
        after = high[g + 1] if g + 1 < len(groups) else zero
        out.append(total_of([
            jnp.where(lane < LY, low[g - 1] if g else zero, low[g]),
            jnp.where(lane >= LANES - LY, after, high[g]),
            jnp.where(lane % LY == 0, 0.0, pltpu.roll(v, 1, 1)),
            jnp.where(lane % LY == LY - 1, 0.0, pltpu.roll(v, LANES - 1, 1)),
            jnp.where(row == 0, 0.0, pltpu.roll(v, 1, 0)),
            jnp.where(row == depth - 1, 0.0, pltpu.roll(v, depth - 1, 0)),
        ]))
    return out


def dot(left, right):
    product = total_of(a * b for a, b in zip(left, right))
    return jnp.sum(jnp.sum(product, axis=0, keepdims=True), axis=1, keepdims=True)


def filtered_column(groups, potential, slow_first, slow_second):
    depth = groups[0].shape[0]
    lane = lax.broadcasted_iota(jnp.int32, (1, LANES), 1)
    field_lane = lax.broadcasted_iota(jnp.int32, (depth, LANES), 1)
    field_row = lax.broadcasted_iota(jnp.int32, (depth, LANES), 0)
    potential = [v * (1.0 / SCALE) for v in potential]
    basis = [groups]
    norms, diagonal, upper = [dot(groups, groups)], [], [None]
    for step in range(DEGREE):
        current = basis[-1]
        norm = norms[-1]
        inverse = jnp.where(norm > 0.0, 1.0 / norm, 0.0)
        image = [
            total * (1.0 / SCALE) - pot * v
            for total, pot, v in zip(neighbour_sum(current, field_lane, field_row), potential, current)
        ]
        if step:
            image = [v - ratio * old for v, old in zip(image, basis[-2])]
        shift = dot(current, image) * inverse
        following = [v - shift * old for v, old in zip(image, current)]
        basis.append(following)
        norms.append(dot(following, following))
        ratio = norms[-1] * inverse
        diagonal.append(SCALE * shift)
        upper.append(SCALE * ratio)
    z_values = shift_constants()
    z = (by_lane(lane, z_values[0]), by_lane(lane, z_values[1]))
    slow = (lane == slow_first) | (lane == slow_second)
    solution_of = solve(norms, diagonal, upper, z, slow)
    weight = (z[0] / NS, z[1] / NS)
    scales = [
        jnp.sum(
            jnp.where(lane < NS, weight[0] * re_part - weight[1] * im_part, 0.0),
            axis=1, keepdims=True,
        )
        for re_part, im_part in solution_of
    ]
    return [
        total_of(scale * v[g] for scale, v in zip(scales, basis)) for g in range(len(groups))
    ]


def kernel(count, cols, sub_ref, pot_ref, slow_ref, out_ref, field, disorder, result,
           own_sem, send_sem, recv_sem, back_send, back_recv):
    me = lax.axis_index("slab")
    planes, cells = pot_ref.shape
    stride = count // cols
    first = lax.axis_index("shift") * cols
    mine = me // stride
    owner = me % stride == 0

    def when_owner(body):
        if stride == 1:
            body()
        else:
            pl.when(owner)(body)

    def outwards(hop):
        column = lax.rem(mine + hop, cols)
        return [
            pltpu.make_async_remote_copy(
                src_ref=source, dst_ref=place.at[me], send_sem=send_sem.at[hop, which],
                recv_sem=recv_sem.at[me, which], device_id={"slab": column * stride},
                device_id_type=MESH,
            )
            for which, (source, place) in enumerate(
                ((sub_ref.at[first + column], field), (pot_ref, disorder))
            )
        ]

    def inwards(offset):
        source = lax.rem(me + offset, count)
        return [
            pltpu.make_async_remote_copy(
                src_ref=place.at[source], dst_ref=place.at[source], send_sem=send_sem.at[0, which],
                recv_sem=recv_sem.at[source, which], device_id={"slab": source},
                device_id_type=MESH,
            )
            for which, place in enumerate((field, disorder))
        ]

    def home(offset):
        target = lax.rem(me + offset, count)
        return pltpu.make_async_remote_copy(
            src_ref=result.at[target], dst_ref=out_ref.at[mine], send_sem=back_send.at[offset],
            recv_sem=back_recv.at[mine], device_id={"slab": target}, device_id_type=MESH,
        )

    def arriving(hop):
        column = lax.rem(mine + hop, cols)
        return pltpu.make_async_remote_copy(
            src_ref=result.at[0], dst_ref=out_ref.at[column], send_sem=back_send.at[0],
            recv_sem=back_recv.at[column], device_id={"slab": column * stride},
            device_id_type=MESH,
        )

    own = [
        pltpu.make_async_copy(sub_ref.at[first + mine], field.at[me], own_sem.at[0]),
        pltpu.make_async_copy(pot_ref, disorder.at[me], own_sem.at[1]),
    ]

    @when_owner
    def _():
        for copy in own:
            copy.start()

    barrier = pltpu.get_barrier_semaphore()
    for offset in range(1, count):
        pl.semaphore_signal(
            barrier, inc=1, device_id={"slab": lax.rem(me + offset, count)}, device_id_type=MESH
        )
    pl.semaphore_wait(barrier, count - 1)

    if stride > 1:
        @pl.when(jnp.logical_not(owner))
        def _():
            for copy in outwards(0):
                copy.start()

    for hop in range(1, cols):
        for copy in outwards(hop):
            copy.start()

    @when_owner
    def _():
        for copy in own:
            copy.wait()
        for offset in range(1, count):
            for copy in inwards(offset):
                copy.wait_recv()
        spans = [slice(g, g + LANES) for g in range(0, cells, LANES)]
        groups = [field[:, :, s].reshape(count * planes, LANES) for s in spans]
        potential = [disorder[:, :, s].reshape(count * planes, LANES) for s in spans]
        answer = filtered_column(groups, potential, slow_ref[0], slow_ref[1])
        for s, value in zip(spans, answer):
            result[:, :, s] = value.reshape(count, planes, LANES)
        keep = pltpu.make_async_copy(result.at[me], out_ref.at[mine], own_sem.at[0])
        keep.start()
        for offset in range(1, count):
            home(offset).start()
        keep.wait()
        for offset in range(1, count):
            home(offset).wait_send()

    if stride > 1:
        @pl.when(jnp.logical_not(owner))
        def _():
            arriving(0).wait_recv()
            for copy in outwards(0):
                copy.wait_send()

    for hop in range(1, cols):
        arriving(hop).wait_recv()
        for copy in outwards(hop):
            copy.wait_send()


def local(subspace, potential, slow_shifts):
    columns, planes, cells = subspace.shape
    count = lax.axis_size("slab")
    cols = columns // lax.axis_size("shift")
    return pl.pallas_call(
        functools.partial(kernel, count, cols),
        out_shape=pltpu.VMEM((cols, planes, cells), jnp.float32),
        in_specs=[
            pl.BlockSpec(memory_space=pl.ANY),
            pl.BlockSpec(memory_space=pl.ANY),
            pl.BlockSpec(memory_space=pltpu.SMEM),
        ],
        out_specs=pl.BlockSpec(memory_space=pltpu.VMEM),
        scratch_shapes=[
            pltpu.VMEM((count, planes, cells), jnp.float32),
            pltpu.VMEM((count, planes, cells), jnp.float32),
            pltpu.VMEM((count, planes, cells), jnp.float32),
            pltpu.SemaphoreType.DMA((2,)),
            pltpu.SemaphoreType.DMA((cols, 2)),
            pltpu.SemaphoreType.DMA((count, 2)),
            pltpu.SemaphoreType.DMA((count,)),
            pltpu.SemaphoreType.DMA((cols,)),
        ],
        compiler_params=pltpu.CompilerParams(collective_id=0, has_side_effects=True),
    )(subspace, potential, slow_shifts)


def solution(mesh):
    return jax.shard_map(
        local,
        mesh=mesh,
        in_specs=(P(None, ("dom", "slab"), None), P(("dom", "slab"), None), P("dom")),
        out_specs=P("shift", ("dom", "slab"), None),
        check_vma=False,
    )
```

```python
import functools
import math

import jax
import jax.numpy as jnp
import numpy as np
from jax import lax
from jax.experimental import pallas as pl
from jax.experimental.pallas import tpu as pltpu
from jax.sharding import PartitionSpec as P

NS = 8
FAST = 2
SLOW = 4
LY = 32
RADIUS = 4.0
SCALE = 4.0
LANES = 128
DEGREE = 2 * SLOW
MESH = pl.DeviceIdType.MESH


def shift_constants():
    angles = (np.arange(NS, dtype=np.float32) + np.float32(0.5)) * np.float32(math.pi / NS)
    return (np.float32(RADIUS) * np.cos(angles), np.float32(RADIUS) * np.sin(angles))


def by_lane(lane, values):
    picked = jnp.full(lane.shape, float(values[0]), jnp.float32)
    for index in range(1, len(values)):
        picked = jnp.where(lane == index, float(values[index]), picked)
    return picked


def cdiv(top, low):
    magnitude = low[0] * low[0] + low[1] * low[1]
    return (
        (top[0] * low[0] + top[1] * low[1]) / magnitude,
        (top[1] * low[0] - top[0] * low[1]) / magnitude,
    )


def cmul(left, right):
    return (left[0] * right[0] - left[1] * right[1], left[0] * right[1] + left[1] * right[0])


def cadd(left, right):
    return (left[0] + right[0], left[1] + right[1])


def csub(left, right):
    return (left[0] - right[0], left[1] - right[1])


def total_of(terms):
    terms = list(terms)
    while len(terms) > 1:
        terms = [
            terms[i] + terms[i + 1] if i + 1 < len(terms) else terms[i]
            for i in range(0, len(terms), 2)
        ]
    return terms[0]


def shifted(poly, z, diagonal, upper):
    count = len(poly)
    out = []
    for j in range(count + 1):
        terms = []
        if j < count:
            terms.append(cmul((z[0] + diagonal[j], z[1]), poly[j]))
        if j >= 1:
            terms.append(tuple(SCALE * part for part in poly[j - 1]))
        if j + 1 < count:
            terms.append(tuple(upper[j + 1] * part for part in poly[j + 1]))
        out.append(tuple(total_of(term[part] for term in terms) for part in (0, 1)))
    return out


def minus(left, factor, right):
    out = []
    for j, value in enumerate(right):
        change = cmul(factor, value)
        out.append(csub(left[j], change) if j < len(left) else (-change[0], -change[1]))
    return out


def solve(norms, diagonal, upper, z, slow):
    zero = jnp.zeros_like(z[0])
    one = jnp.ones_like(z[0])
    solution = [(zero, zero)] * DEGREE
    residual = [(one, zero)]
    search = [(one, zero)]
    for step in range(SLOW):
        image = shifted(search, z, diagonal, upper)
        alpha = cdiv(residual[0], image[0])
        middle = minus(residual, alpha, image)
        second = shifted(middle, z, diagonal, upper)
        heavy = [tuple(norms[j] * part for part in second[j]) for j in range(len(second))]
        pairs = list(zip(heavy, middle))
        ts_re = total_of(s[0] * m[0] + s[1] * m[1] for s, m in pairs)
        ts_im = total_of(s[0] * m[1] - s[1] * m[0] for s, m in pairs)
        t_norm = total_of(h[0] * s[0] + h[1] * s[1] for h, s in zip(heavy, second))
        omega = (ts_re / t_norm, ts_im / t_norm)
        for j in range(len(middle)):
            change = cmul(omega, middle[j])
            if j < len(search):
                change = cadd(change, cmul(alpha, search[j]))
            new = cadd(solution[j], change)
            if step >= FAST:
                new = tuple(jnp.where(slow, a, b) for a, b in zip(new, solution[j]))
            solution[j] = new
        if step == SLOW - 1:
            break
        before = residual[0]
        residual = minus(middle, omega, second)
        beta = cmul(cdiv(residual[0], before), cdiv(alpha, omega))
        inner = minus(search, omega, image)
        search = [
            cadd(residual[j], cmul(beta, inner[j])) if j < len(inner) else residual[j]
            for j in range(len(residual))
        ]
    return solution


def neighbour_sum(groups, lane, row):
    depth = groups[0].shape[0]
    low = [pltpu.roll(v, LY, 1) for v in groups]
    high = [pltpu.roll(v, LANES - LY, 1) for v in groups]
    zero = jnp.zeros_like(groups[0])
    out = []
    for g, v in enumerate(groups):
        after = high[g + 1] if g + 1 < len(groups) else zero
        out.append(total_of([
            jnp.where(lane < LY, low[g - 1] if g else zero, low[g]),
            jnp.where(lane >= LANES - LY, after, high[g]),
            jnp.where(lane % LY == 0, 0.0, pltpu.roll(v, 1, 1)),
            jnp.where(lane % LY == LY - 1, 0.0, pltpu.roll(v, LANES - 1, 1)),
            jnp.where(row == 0, 0.0, pltpu.roll(v, 1, 0)),
            jnp.where(row == depth - 1, 0.0, pltpu.roll(v, depth - 1, 0)),
        ]))
    return out


def dot(left, right):
    product = total_of(a * b for a, b in zip(left, right))
    return jnp.sum(jnp.sum(product, axis=0, keepdims=True), axis=1, keepdims=True)


def filtered_column(groups, potential, slow_first, slow_second):
    depth = groups[0].shape[0]
    lane = lax.broadcasted_iota(jnp.int32, (1, LANES), 1)
    field_lane = lax.broadcasted_iota(jnp.int32, (depth, LANES), 1)
    field_row = lax.broadcasted_iota(jnp.int32, (depth, LANES), 0)
    potential = [v * (1.0 / SCALE) for v in potential]
    basis = [groups]
    norms, diagonal, upper = [dot(groups, groups)], [], [None]
    for step in range(DEGREE):
        current = basis[-1]
        norm = norms[-1]
        inverse = jnp.where(norm > 0.0, 1.0 / norm, 0.0)
        image = [
            total * (1.0 / SCALE) - pot * v
            for total, pot, v in zip(neighbour_sum(current, field_lane, field_row), potential, current)
        ]
        shift = dot(current, image) * inverse
        if step:
            image = [v - ratio * old for v, old in zip(image, basis[-2])]
        following = [v - shift * old for v, old in zip(image, current)]
        basis.append(following)
        norms.append(dot(following, following))
        ratio = norms[-1] * inverse
        diagonal.append(SCALE * shift)
        upper.append(SCALE * ratio)
    z_values = shift_constants()
    z = (by_lane(lane, z_values[0]), by_lane(lane, z_values[1]))
    slow = (lane == slow_first) | (lane == slow_second)
    solution_of = solve(norms, diagonal, upper, z, slow)
    weight = (z[0] / NS, z[1] / NS)
    scales = [
        jnp.sum(
            jnp.where(lane < NS, weight[0] * re_part - weight[1] * im_part, 0.0),
            axis=1, keepdims=True,
        )
        for re_part, im_part in solution_of
    ]
    return [
        total_of(scale * v[g] for scale, v in zip(scales, basis)) for g in range(len(groups))
    ]


def kernel(count, cols, sub_ref, pot_ref, slow_ref, out_ref, field, disorder, result,
           own_sem, send_sem, recv_sem, back_send, back_recv, pair_sem):
    me = lax.axis_index("slab")
    planes, cells = pot_ref.shape
    stride = count // cols
    group = lax.axis_index("shift")
    first = group * cols
    half = cells // 2
    share = pl.ds(pl.multiple_of(lax.rem(group, 2) * half, half), half)
    partner = {"shift": group + 1 - 2 * lax.rem(group, 2)}
    mine = me // stride
    owner = me % stride == 0

    def when_owner(body):
        if stride == 1:
            body()
        else:
            pl.when(owner)(body)

    def outwards(hop):
        column = lax.rem(mine + hop, cols)
        return [
            pltpu.make_async_remote_copy(
                src_ref=source, dst_ref=place, send_sem=send_sem.at[hop, which],
                recv_sem=recv_sem.at[me, which], device_id={"slab": column * stride},
                device_id_type=MESH,
            )
            for which, (source, place) in enumerate(
                (
                    (pot_ref.at[:, share], disorder.at[me, :, share]),
                    (sub_ref.at[first + column], field.at[me]),
                )
            )
        ]

    def inwards(offset, which):
        source = lax.rem(me + offset, count)
        place = field.at[source] if which else disorder.at[source, :, share]
        return pltpu.make_async_remote_copy(
            src_ref=place, dst_ref=place, send_sem=send_sem.at[0, which],
            recv_sem=recv_sem.at[source, which], device_id={"slab": source},
            device_id_type=MESH,
        )

    def paired(lanes):
        return pltpu.make_async_remote_copy(
            src_ref=disorder.at[:, :, lanes], dst_ref=disorder.at[:, :, lanes],
            send_sem=pair_sem.at[0], recv_sem=pair_sem.at[1], device_id=partner,
            device_id_type=MESH,
        )

    def home(offset):
        target = lax.rem(me + offset, count)
        return pltpu.make_async_remote_copy(
            src_ref=result.at[target], dst_ref=out_ref.at[mine], send_sem=back_send.at[offset],
            recv_sem=back_recv.at[mine], device_id={"slab": target}, device_id_type=MESH,
        )

    def arriving(hop):
        column = lax.rem(mine + hop, cols)
        return pltpu.make_async_remote_copy(
            src_ref=result.at[0], dst_ref=out_ref.at[column], send_sem=back_send.at[0],
            recv_sem=back_recv.at[column], device_id={"slab": column * stride},
            device_id_type=MESH,
        )

    own = [
        pltpu.make_async_copy(sub_ref.at[first + mine], field.at[me], own_sem.at[0]),
        pltpu.make_async_copy(pot_ref.at[:, share], disorder.at[me, :, share], own_sem.at[1]),
    ]

    @when_owner
    def _():
        for copy in own:
            copy.start()

    barrier = pltpu.get_barrier_semaphore()
    for offset in range(1, count):
        pl.semaphore_signal(
            barrier, inc=1, device_id={"slab": lax.rem(me + offset, count)}, device_id_type=MESH
        )
    pl.semaphore_signal(barrier, inc=1, device_id=partner, device_id_type=MESH)
    pl.semaphore_wait(barrier, count)

    if stride > 1:
        @pl.when(jnp.logical_not(owner))
        def _():
            for copy in outwards(0):
                copy.start()

    for which in range(2):
        for hop in range(1, cols):
            outwards(hop)[which].start()

    @when_owner
    def _():
        for copy in own:
            copy.wait()
        for offset in range(1, count):
            inwards(offset, 0).wait_recv()
        paired(share).start()
        for offset in range(1, count):
            inwards(offset, 1).wait_recv()
        other = pl.ds(pl.multiple_of(half - lax.rem(group, 2) * half, half), half)
        paired(other).wait_recv()
        spans = [slice(g, g + LANES) for g in range(0, cells, LANES)]
        groups = [field[:, :, s].reshape(count * planes, LANES) for s in spans]
        potential = [disorder[:, :, s].reshape(count * planes, LANES) for s in spans]
        answer = filtered_column(groups, potential, slow_ref[0], slow_ref[1])
        for s, value in zip(spans, answer):
            result[:, :, s] = value.reshape(count, planes, LANES)
        keep = pltpu.make_async_copy(result.at[me], out_ref.at[mine], own_sem.at[0])
        keep.start()
        for offset in range(1, count):
            home(offset).start()
        keep.wait()
        paired(share).wait_send()
        for offset in range(1, count):
            home(offset).wait_send()

    if stride > 1:
        @pl.when(jnp.logical_not(owner))
        def _():
            arriving(0).wait_recv()
            for copy in outwards(0):
                copy.wait_send()

    for hop in range(1, cols):
        arriving(hop).wait_recv()
        for copy in outwards(hop):
            copy.wait_send()


def local(subspace, potential, slow_shifts):
    columns, planes, cells = subspace.shape
    count = lax.axis_size("slab")
    cols = columns // lax.axis_size("shift")
    return pl.pallas_call(
        functools.partial(kernel, count, cols),
        out_shape=pltpu.VMEM((cols, planes, cells), jnp.float32),
        in_specs=[
            pl.BlockSpec(memory_space=pl.ANY),
            pl.BlockSpec(memory_space=pl.ANY),
            pl.BlockSpec(memory_space=pltpu.SMEM),
        ],
        out_specs=pl.BlockSpec(memory_space=pltpu.VMEM),
        scratch_shapes=[
            pltpu.VMEM((count, planes, cells), jnp.float32),
            pltpu.VMEM((count, planes, cells), jnp.float32),
            pltpu.VMEM((count, planes, cells), jnp.float32),
            pltpu.SemaphoreType.DMA((2,)),
            pltpu.SemaphoreType.DMA((cols, 2)),
            pltpu.SemaphoreType.DMA((count, 2)),
            pltpu.SemaphoreType.DMA((count,)),
            pltpu.SemaphoreType.DMA((cols,)),
            pltpu.SemaphoreType.DMA((2,)),
        ],
        compiler_params=pltpu.CompilerParams(collective_id=0, has_side_effects=True),
    )(subspace, potential, slow_shifts)


def solution(mesh):
    return jax.shard_map(
        local,
        mesh=mesh,
        in_specs=(P(None, ("dom", "slab"), None), P(("dom", "slab"), None), P("dom")),
        out_specs=P("shift", ("dom", "slab"), None),
        check_vma=False,
    )
```

```python
import functools
import math

import jax
import jax.numpy as jnp
import numpy as np
from jax import lax
from jax.experimental import pallas as pl
from jax.experimental.pallas import tpu as pltpu
from jax.sharding import PartitionSpec as P

NS = 8
FAST = 2
SLOW = 4
LY = 32
RADIUS = 4.0
SCALE = 4.0
LANES = 128
DEGREE = 2 * SLOW
MESH = pl.DeviceIdType.MESH


def shift_constants():
    angles = (np.arange(NS, dtype=np.float32) + np.float32(0.5)) * np.float32(math.pi / NS)
    return (np.float32(RADIUS) * np.cos(angles), np.float32(RADIUS) * np.sin(angles))


def by_lane(lane, values):
    picked = jnp.full(lane.shape, float(values[0]), jnp.float32)
    for index in range(1, len(values)):
        picked = jnp.where(lane == index, float(values[index]), picked)
    return picked


def cdiv(top, low):
    magnitude = low[0] * low[0] + low[1] * low[1]
    return (
        (top[0] * low[0] + top[1] * low[1]) / magnitude,
        (top[1] * low[0] - top[0] * low[1]) / magnitude,
    )


def cmul(left, right):
    return (left[0] * right[0] - left[1] * right[1], left[0] * right[1] + left[1] * right[0])


def cadd(left, right):
    return (left[0] + right[0], left[1] + right[1])


def csub(left, right):
    return (left[0] - right[0], left[1] - right[1])


def total_of(terms):
    terms = list(terms)
    while len(terms) > 1:
        terms = [
            terms[i] + terms[i + 1] if i + 1 < len(terms) else terms[i]
            for i in range(0, len(terms), 2)
        ]
    return terms[0]


def shifted(poly, z, diagonal, upper):
    count = len(poly)
    out = []
    for j in range(count + 1):
        terms = []
        if j < count:
            terms.append(cmul((z[0] + diagonal[j], z[1]), poly[j]))
        if j >= 1:
            terms.append(tuple(SCALE * part for part in poly[j - 1]))
        if j + 1 < count:
            terms.append(tuple(upper[j + 1] * part for part in poly[j + 1]))
        out.append(tuple(total_of(term[part] for term in terms) for part in (0, 1)))
    return out


def minus(left, factor, right):
    out = []
    for j, value in enumerate(right):
        change = cmul(factor, value)
        out.append(csub(left[j], change) if j < len(left) else (-change[0], -change[1]))
    return out


def solve(norms, diagonal, upper, z, slow):
    zero = jnp.zeros_like(z[0])
    one = jnp.ones_like(z[0])
    solution = [(zero, zero)] * DEGREE
    residual = [(one, zero)]
    search = [(one, zero)]
    for step in range(SLOW):
        image = shifted(search, z, diagonal, upper)
        alpha = cdiv(residual[0], image[0])
        middle = minus(residual, alpha, image)
        second = shifted(middle, z, diagonal, upper)
        heavy = [tuple(norms[j] * part for part in second[j]) for j in range(len(second))]
        pairs = list(zip(heavy, middle))
        ts_re = total_of(s[0] * m[0] + s[1] * m[1] for s, m in pairs)
        ts_im = total_of(s[0] * m[1] - s[1] * m[0] for s, m in pairs)
        t_norm = total_of(h[0] * s[0] + h[1] * s[1] for h, s in zip(heavy, second))
        omega = (ts_re / t_norm, ts_im / t_norm)
        for j in range(len(middle)):
            change = cmul(omega, middle[j])
            if j < len(search):
                change = cadd(change, cmul(alpha, search[j]))
            new = cadd(solution[j], change)
            if step >= FAST:
                new = tuple(jnp.where(slow, a, b) for a, b in zip(new, solution[j]))
            solution[j] = new
        if step == SLOW - 1:
            break
        before = residual[0]
        residual = minus(middle, omega, second)
        beta = cmul(cdiv(residual[0], before), cdiv(alpha, omega))
        inner = minus(search, omega, image)
        search = [
            cadd(residual[j], cmul(beta, inner[j])) if j < len(inner) else residual[j]
            for j in range(len(residual))
        ]
    return solution


def neighbour_sum(groups, lane, row):
    depth = groups[0].shape[0]
    low = [pltpu.roll(v, LY, 1) for v in groups]
    high = [pltpu.roll(v, LANES - LY, 1) for v in groups]
    zero = jnp.zeros_like(groups[0])
    out = []
    for g, v in enumerate(groups):
        after = high[g + 1] if g + 1 < len(groups) else zero
        out.append(total_of([
            jnp.where(lane < LY, low[g - 1] if g else zero, low[g]),
            jnp.where(lane >= LANES - LY, after, high[g]),
            jnp.where(lane % LY == 0, 0.0, pltpu.roll(v, 1, 1)),
            jnp.where(lane % LY == LY - 1, 0.0, pltpu.roll(v, LANES - 1, 1)),
            jnp.where(row == 0, 0.0, pltpu.roll(v, 1, 0)),
            jnp.where(row == depth - 1, 0.0, pltpu.roll(v, depth - 1, 0)),
        ]))
    return out


def dot(left, right):
    product = total_of(a * b for a, b in zip(left, right))
    return jnp.sum(jnp.sum(product, axis=0, keepdims=True), axis=1, keepdims=True)


def filtered_column(groups, potential, slow_first, slow_second):
    depth = groups[0].shape[0]
    lane = lax.broadcasted_iota(jnp.int32, (1, LANES), 1)
    field_lane = lax.broadcasted_iota(jnp.int32, (depth, LANES), 1)
    field_row = lax.broadcasted_iota(jnp.int32, (depth, LANES), 0)
    potential = [v * (1.0 / SCALE) for v in potential]
    basis = [groups]
    norms, diagonal, upper = [dot(groups, groups)], [], [None]
    for step in range(DEGREE):
        current = basis[-1]
        norm = norms[-1]
        inverse = jnp.where(norm > 0.0, 1.0 / norm, 0.0)
        image = [
            total * (1.0 / SCALE) - pot * v
            for total, pot, v in zip(neighbour_sum(current, field_lane, field_row), potential, current)
        ]
        shift = dot(current, image) * inverse
        if step:
            image = [v - ratio * old for v, old in zip(image, basis[-2])]
        following = [v - shift * old for v, old in zip(image, current)]
        basis.append(following)
        norms.append(dot(following, following))
        ratio = norms[-1] * inverse
        diagonal.append(SCALE * shift)
        upper.append(SCALE * ratio)
    z_values = shift_constants()
    z = (by_lane(lane, z_values[0]), by_lane(lane, z_values[1]))
    slow = (lane == slow_first) | (lane == slow_second)
    solution_of = solve(norms, diagonal, upper, z, slow)
    weight = (z[0] / NS, z[1] / NS)
    scales = [
        jnp.sum(
            jnp.where(lane < NS, weight[0] * re_part - weight[1] * im_part, 0.0),
            axis=1, keepdims=True,
        )
        for re_part, im_part in solution_of
    ]
    return [
        total_of(scale * v[g] for scale, v in zip(scales, basis)) for g in range(len(groups))
    ]


def kernel(count, cols, sub_ref, pot_ref, slow_ref, out_ref, field, disorder, result,
           own_sem, send_sem, recv_sem, back_send, back_recv, pair_sem,
           staged, staged_pot):
    me = lax.axis_index("slab")
    planes, cells = pot_ref.shape
    stride = count // cols
    group = lax.axis_index("shift")
    first = group * cols
    half = cells // 2
    share = pl.ds(pl.multiple_of(lax.rem(group, 2) * half, half), half)
    partner = {"shift": group + 1 - 2 * lax.rem(group, 2)}
    mine = me // stride
    owner = me % stride == 0

    def when_owner(body):
        if stride == 1:
            body()
        else:
            pl.when(owner)(body)

    def outwards(hop):
        column = lax.rem(mine + hop, cols)
        return [
            pltpu.make_async_remote_copy(
                src_ref=source, dst_ref=place, send_sem=send_sem.at[hop, which],
                recv_sem=recv_sem.at[me, which], device_id={"slab": column * stride},
                device_id_type=MESH,
            )
            for which, (source, place) in enumerate(
                (
                    (staged_pot.at[:, share], disorder.at[me, :, share]),
                    (staged.at[column], field.at[me]),
                )
            )
        ]

    def inwards(offset, which):
        source = lax.rem(me + offset, count)
        place = field.at[source] if which else disorder.at[source, :, share]
        return pltpu.make_async_remote_copy(
            src_ref=place, dst_ref=place, send_sem=send_sem.at[0, which],
            recv_sem=recv_sem.at[source, which], device_id={"slab": source},
            device_id_type=MESH,
        )

    def paired(lanes):
        return pltpu.make_async_remote_copy(
            src_ref=disorder.at[:, :, lanes], dst_ref=disorder.at[:, :, lanes],
            send_sem=pair_sem.at[0], recv_sem=pair_sem.at[1], device_id=partner,
            device_id_type=MESH,
        )

    def home(offset):
        target = lax.rem(me + offset, count)
        return pltpu.make_async_remote_copy(
            src_ref=result.at[target], dst_ref=out_ref.at[mine], send_sem=back_send.at[offset],
            recv_sem=back_recv.at[mine], device_id={"slab": target}, device_id_type=MESH,
        )

    def arriving(hop):
        column = lax.rem(mine + hop, cols)
        return pltpu.make_async_remote_copy(
            src_ref=result.at[0], dst_ref=out_ref.at[column], send_sem=back_send.at[0],
            recv_sem=back_recv.at[column], device_id={"slab": column * stride},
            device_id_type=MESH,
        )

    own = [
        pltpu.make_async_copy(sub_ref.at[first + mine], field.at[me], own_sem.at[0]),
        pltpu.make_async_copy(pot_ref.at[:, share], disorder.at[me, :, share], own_sem.at[1]),
    ]

    stage = [
        pltpu.make_async_copy(sub_ref.at[pl.ds(first, cols)], staged, own_sem.at[2]),
        pltpu.make_async_copy(pot_ref, staged_pot, own_sem.at[3]),
    ]
    for copy in stage:
        copy.start()

    @when_owner
    def _():
        for copy in own:
            copy.start()

    barrier = pltpu.get_barrier_semaphore()
    for offset in range(1, count):
        pl.semaphore_signal(
            barrier, inc=1, device_id={"slab": lax.rem(me + offset, count)}, device_id_type=MESH
        )
    pl.semaphore_signal(barrier, inc=1, device_id=partner, device_id_type=MESH)
    for copy in stage:
        copy.wait()
    pl.semaphore_wait(barrier, count)

    if stride > 1:
        @pl.when(jnp.logical_not(owner))
        def _():
            for copy in outwards(0):
                copy.start()

    for which in range(2):
        for hop in range(1, cols):
            outwards(hop)[which].start()

    @when_owner
    def _():
        for copy in own:
            copy.wait()
        for offset in range(1, count):
            inwards(offset, 0).wait_recv()
        paired(share).start()
        for offset in range(1, count):
            inwards(offset, 1).wait_recv()
        other = pl.ds(pl.multiple_of(half - lax.rem(group, 2) * half, half), half)
        paired(other).wait_recv()
        spans = [slice(g, g + LANES) for g in range(0, cells, LANES)]
        groups = [field[:, :, s].reshape(count * planes, LANES) for s in spans]
        potential = [disorder[:, :, s].reshape(count * planes, LANES) for s in spans]
        answer = filtered_column(groups, potential, slow_ref[0], slow_ref[1])
        for s, value in zip(spans, answer):
            result[:, :, s] = value.reshape(count, planes, LANES)
        keep = pltpu.make_async_copy(result.at[me], out_ref.at[mine], own_sem.at[0])
        keep.start()
        for offset in range(1, count):
            home(offset).start()
        keep.wait()
        paired(share).wait_send()
        for offset in range(1, count):
            home(offset).wait_send()

    if stride > 1:
        @pl.when(jnp.logical_not(owner))
        def _():
            arriving(0).wait_recv()
            for copy in outwards(0):
                copy.wait_send()

    for hop in range(1, cols):
        arriving(hop).wait_recv()
        for copy in outwards(hop):
            copy.wait_send()


def local(subspace, potential, slow_shifts):
    columns, planes, cells = subspace.shape
    count = lax.axis_size("slab")
    cols = columns // lax.axis_size("shift")
    return pl.pallas_call(
        functools.partial(kernel, count, cols),
        out_shape=pltpu.VMEM((cols, planes, cells), jnp.float32),
        in_specs=[
            pl.BlockSpec(memory_space=pl.ANY),
            pl.BlockSpec(memory_space=pl.ANY),
            pl.BlockSpec(memory_space=pltpu.SMEM),
        ],
        out_specs=pl.BlockSpec(memory_space=pltpu.VMEM),
        scratch_shapes=[
            pltpu.VMEM((count, planes, cells), jnp.float32),
            pltpu.VMEM((count, planes, cells), jnp.float32),
            pltpu.VMEM((count, planes, cells), jnp.float32),
            pltpu.SemaphoreType.DMA((4,)),
            pltpu.SemaphoreType.DMA((cols, 2)),
            pltpu.SemaphoreType.DMA((count, 2)),
            pltpu.SemaphoreType.DMA((count,)),
            pltpu.SemaphoreType.DMA((cols,)),
            pltpu.SemaphoreType.DMA((2,)),
            pltpu.VMEM((cols, planes, cells), jnp.float32),
            pltpu.VMEM((planes, cells), jnp.float32),
        ],
        compiler_params=pltpu.CompilerParams(collective_id=0, has_side_effects=True),
    )(subspace, potential, slow_shifts)


def solution(mesh):
    return jax.shard_map(
        local,
        mesh=mesh,
        in_specs=(P(None, ("dom", "slab"), None), P(("dom", "slab"), None), P("dom")),
        out_specs=P("shift", ("dom", "slab"), None),
        check_vma=False,
    )
```

```python
import functools
import math

import jax
import jax.numpy as jnp
import numpy as np
from jax import lax
from jax.experimental import pallas as pl
from jax.experimental.pallas import tpu as pltpu
from jax.sharding import PartitionSpec as P

NS = 8
FAST = 2
SLOW = 4
LY = 32
RADIUS = 4.0
SCALE = 4.0
LANES = 128
DEGREE = 2 * SLOW
MESH = pl.DeviceIdType.MESH


def shift_constants():
    angles = (np.arange(NS, dtype=np.float32) + np.float32(0.5)) * np.float32(math.pi / NS)
    return (np.float32(RADIUS) * np.cos(angles), np.float32(RADIUS) * np.sin(angles))


def by_lane(lane, values):
    picked = jnp.full(lane.shape, float(values[0]), jnp.float32)
    for index in range(1, len(values)):
        picked = jnp.where(lane == index, float(values[index]), picked)
    return picked


def cdiv(top, low):
    magnitude = low[0] * low[0] + low[1] * low[1]
    return (
        (top[0] * low[0] + top[1] * low[1]) / magnitude,
        (top[1] * low[0] - top[0] * low[1]) / magnitude,
    )


def cmul(left, right):
    return (left[0] * right[0] - left[1] * right[1], left[0] * right[1] + left[1] * right[0])


def cadd(left, right):
    return (left[0] + right[0], left[1] + right[1])


def csub(left, right):
    return (left[0] - right[0], left[1] - right[1])


def total_of(terms):
    terms = list(terms)
    while len(terms) > 1:
        terms = [
            terms[i] + terms[i + 1] if i + 1 < len(terms) else terms[i]
            for i in range(0, len(terms), 2)
        ]
    return terms[0]


def shifted(poly, z, diagonal, upper):
    count = len(poly)
    out = []
    for j in range(count + 1):
        terms = []
        if j < count:
            terms.append(cmul((z[0] + diagonal[j], z[1]), poly[j]))
        if j >= 1:
            terms.append(tuple(SCALE * part for part in poly[j - 1]))
        if j + 1 < count:
            terms.append(tuple(upper[j + 1] * part for part in poly[j + 1]))
        out.append(tuple(total_of(term[part] for term in terms) for part in (0, 1)))
    return out


def minus(left, factor, right):
    out = []
    for j, value in enumerate(right):
        change = cmul(factor, value)
        out.append(csub(left[j], change) if j < len(left) else (-change[0], -change[1]))
    return out


def solve(norms, diagonal, upper, z, slow):
    zero = jnp.zeros_like(z[0])
    one = jnp.ones_like(z[0])
    solution = [(zero, zero)] * DEGREE
    residual = [(one, zero)]
    search = [(one, zero)]
    for step in range(SLOW):
        image = shifted(search, z, diagonal, upper)
        alpha = cdiv(residual[0], image[0])
        middle = minus(residual, alpha, image)
        second = shifted(middle, z, diagonal, upper)
        heavy = [tuple(norms[j] * part for part in second[j]) for j in range(len(second))]
        pairs = list(zip(heavy, middle))
        ts_re = total_of(s[0] * m[0] + s[1] * m[1] for s, m in pairs)
        ts_im = total_of(s[0] * m[1] - s[1] * m[0] for s, m in pairs)
        t_norm = total_of(h[0] * s[0] + h[1] * s[1] for h, s in zip(heavy, second))
        omega = (ts_re / t_norm, ts_im / t_norm)
        for j in range(len(middle)):
            change = cmul(omega, middle[j])
            if j < len(search):
                change = cadd(change, cmul(alpha, search[j]))
            new = cadd(solution[j], change)
            if step >= FAST:
                new = tuple(jnp.where(slow, a, b) for a, b in zip(new, solution[j]))
            solution[j] = new
        if step == SLOW - 1:
            break
        before = residual[0]
        residual = minus(middle, omega, second)
        beta = cmul(cdiv(residual[0], before), cdiv(alpha, omega))
        inner = minus(search, omega, image)
        search = [
            cadd(residual[j], cmul(beta, inner[j])) if j < len(inner) else residual[j]
            for j in range(len(residual))
        ]
    return solution


def neighbour_sum(groups, lane, row):
    depth = groups[0].shape[0]
    low = [pltpu.roll(v, LY, 1) for v in groups]
    high = [pltpu.roll(v, LANES - LY, 1) for v in groups]
    zero = jnp.zeros_like(groups[0])
    out = []
    for g, v in enumerate(groups):
        after = high[g + 1] if g + 1 < len(groups) else zero
        out.append(total_of([
            jnp.where(lane < LY, low[g - 1] if g else zero, low[g]),
            jnp.where(lane >= LANES - LY, after, high[g]),
            jnp.where(lane % LY == 0, 0.0, pltpu.roll(v, 1, 1)),
            jnp.where(lane % LY == LY - 1, 0.0, pltpu.roll(v, LANES - 1, 1)),
            jnp.concatenate([zero[:1], v[:-1]], 0),
            jnp.concatenate([v[1:], zero[:1]], 0),
        ]))
    return out


def dot(left, right):
    product = total_of(a * b for a, b in zip(left, right))
    return jnp.sum(jnp.sum(product, axis=0, keepdims=True), axis=1, keepdims=True)


def filtered_column(groups, potential, slow_first, slow_second):
    depth = groups[0].shape[0]
    lane = lax.broadcasted_iota(jnp.int32, (1, LANES), 1)
    field_lane = lax.broadcasted_iota(jnp.int32, (depth, LANES), 1)
    field_row = lax.broadcasted_iota(jnp.int32, (depth, LANES), 0)
    potential = [v * (1.0 / SCALE) for v in potential]
    basis = [groups]
    norms, diagonal, upper = [dot(groups, groups)], [], [None]
    for step in range(DEGREE):
        current = basis[-1]
        norm = norms[-1]
        inverse = jnp.where(norm > 0.0, 1.0 / norm, 0.0)
        image = [
            total * (1.0 / SCALE) - pot * v
            for total, pot, v in zip(neighbour_sum(current, field_lane, field_row), potential, current)
        ]
        shift = dot(current, image) * inverse
        if step:
            image = [v - ratio * old for v, old in zip(image, basis[-2])]
        following = [v - shift * old for v, old in zip(image, current)]
        basis.append(following)
        norms.append(dot(following, following))
        ratio = norms[-1] * inverse
        diagonal.append(SCALE * shift)
        upper.append(SCALE * ratio)
    z_values = shift_constants()
    z = (by_lane(lane, z_values[0]), by_lane(lane, z_values[1]))
    slow = (lane == slow_first) | (lane == slow_second)
    solution_of = solve(norms, diagonal, upper, z, slow)
    weight = (z[0] / NS, z[1] / NS)
    scales = [
        jnp.sum(
            jnp.where(lane < NS, weight[0] * re_part - weight[1] * im_part, 0.0),
            axis=1, keepdims=True,
        )
        for re_part, im_part in solution_of
    ]
    return [
        total_of(scale * v[g] for scale, v in zip(scales, basis)) for g in range(len(groups))
    ]


def kernel(count, cols, sub_ref, pot_ref, slow_ref, out_ref, field, disorder, result,
           own_sem, send_sem, recv_sem, back_send, back_recv, pair_sem,
           staged, staged_pot):
    me = lax.axis_index("slab")
    planes, cells = pot_ref.shape
    stride = count // cols
    group = lax.axis_index("shift")
    first = group * cols
    half = cells // 2
    share = pl.ds(pl.multiple_of(lax.rem(group, 2) * half, half), half)
    partner = {"shift": group + 1 - 2 * lax.rem(group, 2)}
    mine = me // stride
    owner = me % stride == 0

    def when_owner(body):
        if stride == 1:
            body()
        else:
            pl.when(owner)(body)

    def outwards(hop):
        column = lax.rem(mine + hop, cols)
        return [
            pltpu.make_async_remote_copy(
                src_ref=source, dst_ref=place, send_sem=send_sem.at[hop, which],
                recv_sem=recv_sem.at[me, which], device_id={"slab": column * stride},
                device_id_type=MESH,
            )
            for which, (source, place) in enumerate(
                (
                    (staged_pot.at[:, share], disorder.at[me, :, share]),
                    (staged.at[column], field.at[me]),
                )
            )
        ]

    def inwards(offset, which):
        source = lax.rem(me + offset, count)
        place = field.at[source] if which else disorder.at[source, :, share]
        return pltpu.make_async_remote_copy(
            src_ref=place, dst_ref=place, send_sem=send_sem.at[0, which],
            recv_sem=recv_sem.at[source, which], device_id={"slab": source},
            device_id_type=MESH,
        )

    def paired(lanes):
        return pltpu.make_async_remote_copy(
            src_ref=disorder.at[:, :, lanes], dst_ref=disorder.at[:, :, lanes],
            send_sem=pair_sem.at[0], recv_sem=pair_sem.at[1], device_id=partner,
            device_id_type=MESH,
        )

    def home(offset):
        target = lax.rem(me + offset, count)
        return pltpu.make_async_remote_copy(
            src_ref=result.at[target], dst_ref=out_ref.at[mine], send_sem=back_send.at[offset],
            recv_sem=back_recv.at[mine], device_id={"slab": target}, device_id_type=MESH,
        )

    def arriving(hop):
        column = lax.rem(mine + hop, cols)
        return pltpu.make_async_remote_copy(
            src_ref=result.at[0], dst_ref=out_ref.at[column], send_sem=back_send.at[0],
            recv_sem=back_recv.at[column], device_id={"slab": column * stride},
            device_id_type=MESH,
        )

    own = [
        pltpu.make_async_copy(sub_ref.at[first + mine], field.at[me], own_sem.at[0]),
        pltpu.make_async_copy(pot_ref.at[:, share], disorder.at[me, :, share], own_sem.at[1]),
    ]

    stage = [
        pltpu.make_async_copy(sub_ref.at[pl.ds(first, cols)], staged, own_sem.at[2]),
        pltpu.make_async_copy(pot_ref, staged_pot, own_sem.at[3]),
    ]
    for copy in stage:
        copy.start()

    @when_owner
    def _():
        for copy in own:
            copy.start()

    barrier = pltpu.get_barrier_semaphore()
    for offset in range(1, count):
        pl.semaphore_signal(
            barrier, inc=1, device_id={"slab": lax.rem(me + offset, count)}, device_id_type=MESH
        )
    pl.semaphore_signal(barrier, inc=1, device_id=partner, device_id_type=MESH)
    for copy in stage:
        copy.wait()
    pl.semaphore_wait(barrier, count)

    if stride > 1:
        @pl.when(jnp.logical_not(owner))
        def _():
            for copy in outwards(0):
                copy.start()

    for which in range(2):
        for hop in sorted(range(1, cols), key=lambda h: abs(2 * h - cols)):
            outwards(hop)[which].start()

    @when_owner
    def _():
        for copy in own:
            copy.wait()
        for offset in range(1, count):
            inwards(offset, 0).wait_recv()
        paired(share).start()
        for offset in range(1, count):
            inwards(offset, 1).wait_recv()
        other = pl.ds(pl.multiple_of(half - lax.rem(group, 2) * half, half), half)
        paired(other).wait_recv()
        spans = [slice(g, g + LANES) for g in range(0, cells, LANES)]
        groups = [field[:, :, s].reshape(count * planes, LANES) for s in spans]
        potential = [disorder[:, :, s].reshape(count * planes, LANES) for s in spans]
        answer = filtered_column(groups, potential, slow_ref[0], slow_ref[1])
        for s, value in zip(spans, answer):
            result[:, :, s] = value.reshape(count, planes, LANES)
        keep = pltpu.make_async_copy(result.at[me], out_ref.at[mine], own_sem.at[0])
        keep.start()
        for offset in range(1, count):
            home(offset).start()
        keep.wait()
        paired(share).wait_send()
        for offset in range(1, count):
            home(offset).wait_send()

    if stride > 1:
        @pl.when(jnp.logical_not(owner))
        def _():
            arriving(0).wait_recv()
            for copy in outwards(0):
                copy.wait_send()

    for hop in range(1, cols):
        arriving(hop).wait_recv()
        for copy in outwards(hop):
            copy.wait_send()


def local(subspace, potential, slow_shifts):
    columns, planes, cells = subspace.shape
    count = lax.axis_size("slab")
    cols = columns // lax.axis_size("shift")
    return pl.pallas_call(
        functools.partial(kernel, count, cols),
        out_shape=pltpu.VMEM((cols, planes, cells), jnp.float32),
        in_specs=[
            pl.BlockSpec(memory_space=pl.ANY),
            pl.BlockSpec(memory_space=pl.ANY),
            pl.BlockSpec(memory_space=pltpu.SMEM),
        ],
        out_specs=pl.BlockSpec(memory_space=pltpu.VMEM),
        scratch_shapes=[
            pltpu.VMEM((count, planes, cells), jnp.float32),
            pltpu.VMEM((count, planes, cells), jnp.float32),
            pltpu.VMEM((count, planes, cells), jnp.float32),
            pltpu.SemaphoreType.DMA((4,)),
            pltpu.SemaphoreType.DMA((cols, 2)),
            pltpu.SemaphoreType.DMA((count, 2)),
            pltpu.SemaphoreType.DMA((count,)),
            pltpu.SemaphoreType.DMA((cols,)),
            pltpu.SemaphoreType.DMA((2,)),
            pltpu.VMEM((cols, planes, cells), jnp.float32),
            pltpu.VMEM((planes, cells), jnp.float32),
        ],
        compiler_params=pltpu.CompilerParams(collective_id=0, has_side_effects=True),
    )(subspace, potential, slow_shifts)


def solution(mesh):
    return jax.shard_map(
        local,
        mesh=mesh,
        in_specs=(P(None, ("dom", "slab"), None), P(("dom", "slab"), None), P("dom")),
        out_specs=P("shift", ("dom", "slab"), None),
        check_vma=False,
    )
```
